512 devices in a mesh: ctx: 64 (over x, z, core), tp: 8 (over y).
Axes of the slice: x: 4, y: 8, z: 8, core: 2. Of those that a mesh axis runs over, the one named last changes fastest.
Arguments:
- queries: bfloat16 [128, 8192], P('ctx', 'tp'), may hold values from -140 to 140
- cache_keys: bfloat16 [65536, 1024], P('ctx', 'tp'), may hold values from -6 to 6
- cache_values: bfloat16 [65536, 1024], P('ctx', 'tp'), may hold values from -6 to 6
- reply_keys: bfloat16 [128, 1024], P('ctx', 'tp'), may hold values from -6 to 6
- reply_values: bfloat16 [128, 1024], P('ctx', 'tp'), may hold values from -6 to 6
- block_prompt: int32 [64], P('ctx'), may hold values from 0 to 1, as said below
- lengths: int32 [4], replicated, may hold values from 1 to 64, 128 in all
- residual: bfloat16 [128, 8192], P(None, 'ctx'), may hold values from -6 to 6
- norm_gain: float32 [8192], P('ctx'), may hold values from 0.5 to 1.5
- out_weight: bfloat16 [8192, 8192], P('tp', 'ctx'), may hold values from -0.0625 to 0.0625
- vocab_weight: bfloat16 [8192, 16384], P('ctx', 'tp'), may hold values from -0.2 to 0.2
- targets: int32 [128], P('ctx'), may hold values from 0 to 16383
Outputs:
- slab_lse: float32 [128], P('ctx')
- target_logit: float32 [128], P('ctx')
The draws below stay inside these ranges and needn't reach their ends.
Inputs may be any that keep to these rules, and one draw needn't show every extreme that they name: `block_prompt`: each prompt owns exactly 32 blocks.
All inputs are finite; a program needn't handle non-finite values.
Results may differ from the reference program's by a relative error of at most 0.0085.
Values may be sent and summed in bfloat16 or wider, within the bound.
A program may use at most 192 MiB of HBM per device.

```python
import math
import jax
import jax.numpy as jnp
import numpy as np
from jax import lax

D = 8192
H = 64
KVH = 8
HD = 128
VOCAB = 16384
CTX_DEV = 1024
RROWS = 128
NBLK = 64
CACHE = 65536


def draw_block_prompt(key, part):
    key = jax.random.fold_in(key, 11)
    order = jax.random.permutation(key, NBLK)
    return (order % 2).astype(jnp.int32)


def draw_queries(key, part):
    key = jax.random.fold_in(key, 5)
    first = jax.random.fold_in(key, 0)
    shape = (RROWS, H * HD)
    values = jnp.clip(jax.random.normal(first, shape, jnp.float32), -6.0, 6.0)
    return values.astype(jnp.bfloat16)


def draw_residual(key, part):
    key = jax.random.fold_in(key, 23)
    values = jnp.clip(jax.random.normal(key, (RROWS, D), jnp.float32), -6.0, 6.0)
    return values.astype(jnp.bfloat16)


def draw_vocab_weight(key, part):
    key = jax.random.fold_in(key, 37)
    first = jax.random.fold_in(key, 0)
    values = jnp.clip(0.035 * jax.random.normal(first, (D, VOCAB), jnp.float32), -0.2, 0.2)
    return values.astype(jnp.bfloat16)


def with_ends(drawn, rng, low, top_value):
    longest = drawn.shape.index(max(drawn.shape))
    spots = []
    for shift in (0, 1):
        where = [jax.random.randint(jax.random.fold_in(rng, axis), (), 0, length) for axis, length in enumerate(drawn.shape)]
        where[longest] = (where[longest] + shift) % drawn.shape[longest]
        spots.append(tuple(where))
    return drawn.at[spots[0]].set(low).at[spots[1]].set(top_value)


def levels(key, shape, pieces, low, top_value):
    gain = 1.0
    for dim, blocks in pieces:
        heights = jax.random.uniform(jax.random.fold_in(jax.random.fold_in(key, 6), dim), (blocks,), jnp.float32, low / len(pieces), top_value / len(pieces))
        gain = gain * jnp.repeat(jnp.exp(heights), shape[dim] // blocks).reshape((-1,) + (1,) * (len(shape) - 1 - dim))
    return gain


def split_up(count, total, most, skew):
    weights = [(1 << 20) // math.isqrt(standing ** skew) + 1 for standing in range(2, count + 1)]
    spare, holding = total - most - (count - 1), [1] * (count - 1)
    while spare > 0:
        movable = [i for i in range(count - 1) if holding[i] < most]
        mass, remaining = sum([weights[i] for i in movable]), spare
        for i in movable:
            more = min(most - holding[i], max(1, remaining * weights[i] // mass), spare)
            holding[i] = holding[i] + more
            spare = spare - more
    return np.array([most] + holding)


def uneven_parts(rng, amount, total, reach, skew):
    if amount == 2:
        one = jax.random.randint(rng, (), max(1, total - reach), min(reach, total - 1) + 1)
        return jnp.stack([one, total - one])
    tallies = jnp.asarray(split_up(amount, total, reach, skew), jnp.int32)
    twos = (amount - 1) // 2
    donor, taker = tallies[1:1 + 2 * twos:2], tallies[2:2 + 2 * twos:2]
    slack = jnp.minimum(donor - 1, reach - taker)
    shifted = jax.random.randint(jax.random.fold_in(rng, 1), (twos,), 0, 1 << 20) % (slack + 1)
    tallies = tallies.at[1:1 + 2 * twos:2].set(donor - shifted).at[2:2 + 2 * twos:2].set(taker + shifted)
    return tallies[jax.random.permutation(jax.random.fold_in(rng, 2), amount)]


def normal_values(key, dims, deviation, bound, shards=(), held_as=jnp.bfloat16):
    drawn = deviation * jax.random.normal(key, dims, jnp.float32)
    if shards:
        drawn = drawn * levels(key, dims, shards, -0.22, 0.18)
    return jnp.clip(drawn, -bound, bound).astype(held_as)


def setup_inputs(seed: int = 0) -> dict:
    splits = jax.random.split(jax.random.key(seed), 13)
    queries = draw_queries(jax.random.fold_in(splits[12], 71), 0)
    cache_keys = normal_values(splits[1], (CACHE, KVH * HD), 1.0, 6.0, ((0, 64), (1, 8)))
    cache_values = normal_values(splits[2], (CACHE, KVH * HD), 1.0, 6.0, ((0, 64), (1, 8)))
    reply_keys = normal_values(splits[3], (RROWS, KVH * HD), 1.0, 6.0, ((0, 64), (1, 8)))
    reply_values = normal_values(splits[4], (RROWS, KVH * HD), 1.0, 6.0, ((0, 64), (1, 8)))
    block_prompt = draw_block_prompt(jax.random.fold_in(splits[12], 71), 0)
    lengths = uneven_parts(splits[6], 4, RROWS, RROWS // 2, 2).astype(jnp.int32)
    residual = draw_residual(jax.random.fold_in(splits[12], 71), 0)
    norm_gain = jnp.clip(1.0 + 0.1 * jax.random.normal(splits[8], (D,), jnp.float32), 0.5, 1.5)
    out_weight = normal_values(splits[9], (H * HD, D), (H * HD) ** -0.5, 0.0625, ((0, 8), (1, 64)))
    vocab_weight = draw_vocab_weight(jax.random.fold_in(splits[12], 71), 0)
    targets = with_ends(jax.random.randint(splits[11], (RROWS,), 0, VOCAB), jax.random.fold_in(splits[11], 1), 0, VOCAB - 1).astype(jnp.int32)
    return dict(queries=queries, cache_keys=cache_keys, cache_values=cache_values, reply_keys=reply_keys, reply_values=reply_values, block_prompt=block_prompt, lengths=lengths, residual=residual, norm_gain=norm_gain, out_weight=out_weight, vocab_weight=vocab_weight, targets=targets)


NEG = -1e+30
EPS = 1e-06

def reference(queries, cache_keys, cache_values, reply_keys, reply_values, block_prompt, lengths, residual, norm_gain, out_weight, vocab_weight, targets):
    ends = jnp.cumsum(lengths)
    rows = jnp.arange(RROWS, dtype=jnp.int32)
    segment = lax.optimization_barrier(jnp.sum((rows[:, None] >= ends[None, :]).astype(jnp.int32), axis=1))
    prompt = segment // 2
    key_prompt = jnp.repeat(block_prompt, CTX_DEV)
    cache_mask = prompt[:, None] == key_prompt[None, :]
    reply_mask = (segment[:, None] == segment[None, :]) & (rows[None, :] <= rows[:, None])
    query_f = queries.astype(jnp.float32)
    ckeys = cache_keys.astype(jnp.float32)
    cvals = cache_values.astype(jnp.float32)
    rkeys = reply_keys.astype(jnp.float32)
    rvals = reply_values.astype(jnp.float32)
    scale = HD ** (-0.5)
    group = H // KVH

    def one_head(index):
        query = lax.dynamic_slice_in_dim(query_f, index * HD, HD, 1)
        column = index // group * HD
        keys = lax.dynamic_slice_in_dim(ckeys, column, HD, 1)
        vals = lax.dynamic_slice_in_dim(cvals, column, HD, 1)
        own_keys = lax.dynamic_slice_in_dim(rkeys, column, HD, 1)
        own_vals = lax.dynamic_slice_in_dim(rvals, column, HD, 1)
        first = jnp.where(cache_mask, jnp.dot(query, keys.T) * scale, NEG)
        second = jnp.where(reply_mask, jnp.dot(query, own_keys.T) * scale, NEG)
        top = jnp.maximum(lax.optimization_barrier(jnp.max(first, axis=1)), lax.optimization_barrier(jnp.max(second, axis=1)))
        pfirst = jnp.where(cache_mask, jnp.exp(first - top[:, None]), 0.0)
        psecond = jnp.where(reply_mask, jnp.exp(second - top[:, None]), 0.0)
        total = lax.optimization_barrier(jnp.sum(pfirst, axis=1)) + lax.optimization_barrier(jnp.sum(psecond, axis=1))
        wfirst = pfirst.astype(jnp.bfloat16).astype(jnp.float32)
        wsecond = psecond.astype(jnp.bfloat16).astype(jnp.float32)
        acc = jnp.dot(wfirst, vals) + jnp.dot(wsecond, own_vals)
        return (acc / total[:, None]).astype(jnp.bfloat16)
    attention = lax.map(one_head, jnp.arange(H, dtype=jnp.int32))
    weight = out_weight.astype(jnp.float32).reshape(H, HD, D)
    mixed = jnp.einsum('hrd,hdc->rc', attention.astype(jnp.float32), weight)
    hidden = residual.astype(jnp.float32) + mixed
    msq = lax.optimization_barrier(jnp.mean(hidden * hidden, axis=1))
    normed = (hidden * lax.rsqrt(msq + EPS)[:, None] * norm_gain[None, :]).astype(jnp.bfloat16)
    logits = jnp.dot(normed, vocab_weight, preferred_element_type=jnp.float32)
    top = lax.optimization_barrier(jnp.max(logits, axis=1))
    slab_lse = top + jnp.log(lax.optimization_barrier(jnp.sum(jnp.exp(logits - top[:, None]), axis=1)))
    columns = jnp.arange(VOCAB, dtype=jnp.int32)
    target_logit = lax.optimization_barrier(jnp.sum(jnp.where(columns[None, :] == targets[:, None], logits, 0.0), axis=1))
    return (slab_lse, target_logit)
```

```python
import functools

import jax
import jax.numpy as jnp
from jax import lax
from jax.experimental import pallas as pl
from jax.experimental.pallas import tpu as pltpu
from jax.sharding import PartitionSpec as P

MESH = pl.DeviceIdType.MESH
F32 = jnp.float32
BF16 = jnp.bfloat16

HD = 128
HEADS = 8
NEG = -1e30
EPS = 1e-06
LOG2E = 1.4426950408889634
LANES = 128
CHUNK = 128


def iota(shape, dim):
    return lax.broadcasted_iota(jnp.int32, shape, dim)


def dot(a, b):
    return jnp.dot(a, b, preferred_element_type=F32)


def dot_t(a, b):
    return lax.dot_general(a, b, (((1,), (1,)), ((), ())), preferred_element_type=F32)


def roll_rows(x, shift, period):
    if shift % period == 0:
        return x
    shift = shift % period
    return jnp.concatenate([x[:, shift:], x[:, :shift]], axis=1)


def kernel(
    plane,
    ny,
    width,
    q_hbm,
    k_hbm,
    v_hbm,
    rk_hbm,
    rv_hbm,
    bp_smem,
    len_smem,
    res_hbm,
    gain_hbm,
    w_hbm,
    vw_hbm,
    tgt_smem,
    out_ref,
    q_in,
    rk_in,
    rv_in,
    gain_in,
    kbuf,
    vbuf,
    resbuf,
    wbuf,
    vwbuf,
    misc,
    qbuf,
    tsrc,
    tbuf,
    perm,
    acc_s,
    acc_r,
    st_s,
    st_r,
    abuf,
    t_s,
    t_r,
    hbuf,
    l_s,
    l_r,
    s2_s,
    s2_r,
    f_r,
    local_sem,
    send_sem,
    recv_sem,
):
    ctx = lax.axis_index("ctx")
    y = lax.axis_index("tp")
    core = ctx % 2
    me = ctx // 2
    partner = (ctx + 1 - 2 * core, y)
    nctx = 2 * plane
    rows = 2 * plane
    qrows = 16 * plane
    groups = plane // 4
    features = nctx * LANES
    keys = kbuf.shape[1]
    c1 = (HD ** (-0.5)) * LOG2E

    def plane_peers():
        return [((ctx + 2 * k) % nctx, y) for k in range(1, plane)]

    def y_peers():
        return [(ctx, (y + k) % ny) for k in range(1, ny)]

    barrier = pltpu.get_barrier_semaphore()
    greeted = [partner] + plane_peers() + y_peers()
    for peer in greeted:
        pl.semaphore_signal(barrier, inc=1, device_id=peer, device_id_type=MESH)

    def local(index, src, dst):
        copy = pltpu.make_async_copy(src, dst, local_sem.at[index])
        copy.start()
        return copy

    copies = [
        local(0, q_hbm, q_in),
        local(1, rk_hbm, rk_in),
        local(2, rv_hbm, rv_in),
        local(3, gain_hbm, gain_in),
    ]
    big = [
        local(4, k_hbm, kbuf.at[0]),
        local(5, v_hbm, vbuf.at[0]),
        local(6, res_hbm, resbuf.at[0]),
        local(7, w_hbm, wbuf.at[0]),
        local(8, vw_hbm, vwbuf.at[0:LANES]),
    ]
    for copy in copies:
        copy.wait()

    def send(index, src, dst, peer):
        pltpu.make_async_remote_copy(
            src_ref=src,
            dst_ref=dst,
            send_sem=send_sem.at[index],
            recv_sem=recv_sem.at[index],
            device_id=peer,
            device_id_type=MESH,
        ).start()

    def bytes_of(index, ref):
        return pltpu.make_async_remote_copy(
            src_ref=ref,
            dst_ref=ref,
            send_sem=send_sem.at[index],
            recv_sem=recv_sem.at[index],
            device_id=partner,
            device_id_type=MESH,
        )

    qf = q_in[...].astype(F32)
    tile = jnp.concatenate([qf[:, h * HD : (h + 1) * HD] for h in range(HEADS)], axis=0)
    qbuf[me] = tile.astype(BF16)
    misc[0, 0:1, :] = gain_in[...]
    misc[0, 1:2, :] = jnp.full((1, LANES), bp_smem[0], jnp.int32).astype(F32)
    misc[0, 2:4, :] = rk_in[...].astype(F32)
    misc[0, 4:6, :] = rv_in[...].astype(F32)
    misc[0, 6:8, :] = jnp.zeros((2, LANES), F32)
    two = iota((2, LANES), 0)
    tsrc[...] = jnp.where(two == 0, tgt_smem[0], tgt_smem[1])
    tbuf[me] = tsrc[...]

    pl.semaphore_wait(barrier, len(greeted))

    for peer in plane_peers():
        send(0, qbuf.at[me], qbuf.at[me], peer)
    send(1, misc.at[0], misc.at[1], partner)
    send(2, k_hbm, kbuf.at[1], partner)
    send(3, v_hbm, vbuf.at[1], partner)
    for peer in plane_peers():
        send(4, tsrc, tbuf.at[me], peer)
    send(5, res_hbm, resbuf.at[1], partner)
    send(6, w_hbm, wbuf.at[1], partner)
    send(7, vw_hbm, vwbuf.at[LANES : 2 * LANES], partner)

    for head in range(HEADS):
        into = iota((rows, qrows), 0)
        source = (into // 2) * 16 + head * 2 + into % 2
        perm[head * rows : (head + 1) * rows, :] = jnp.where(
            iota((rows, qrows), 1) == source, 1.0, 0.0
        ).astype(BF16)

    end0 = len_smem[0]
    end1 = end0 + len_smem[1]
    end2 = end1 + len_smem[2]

    def segment(index):
        one = lambda end: jnp.where(index >= end, 1, 0)
        return one(end0) + one(end1) + one(end2) + one(end2 + len_smem[3])

    for copy in big:
        copy.wait()
    bytes_of(1, misc.at[1]).wait_recv()
    bytes_of(2, kbuf.at[1]).wait_recv()
    bytes_of(3, vbuf.at[1]).wait_recv()

    own, other = misc[0], misc[1]
    fill = jnp.zeros((LANES - 4, HD), F32)
    rk = jnp.concatenate([own[2:4], other[2:4], fill], axis=0).astype(BF16)
    rv = jnp.concatenate([own[4:6], other[4:6], fill], axis=0).astype(BF16)
    prompts = (own[1:2, 0:1], other[1:2, 0:1])
    lane = iota((CHUNK, LANES), 1)
    key_row = jnp.where(lane < 2, 2 * ctx + lane, 2 * (ctx + 1 - 2 * core) + lane - 2)
    key_segment = segment(key_row)

    bytes_of(0, qbuf.at[0 : plane - 1]).wait_recv()

    def attend(chunk):
        first = chunk * CHUNK
        tiles = CHUNK // 16
        q = qbuf[chunk * tiles : (chunk + 1) * tiles].reshape(CHUNK, HD)
        n = first + iota((CHUNK, LANES), 0)
        row = 4 * (n // 16) + 2 * core + n % 2
        row_segment = segment(row)
        row_prompt = (row_segment // 2).astype(F32)
        parts = []
        for block in range(2):
            s = dot_t(q, kbuf[block])
            m = jnp.max(s, axis=1, keepdims=True)
            p = jnp.exp2((s - m) * c1)
            total = jnp.sum(p, axis=1, keepdims=True)
            acc = dot(p.astype(BF16), vbuf[block])
            m = jnp.where(row_prompt == prompts[block], m, NEG)
            parts.append((m, total, acc))
        allowed = (lane < 4) & (key_segment == row_segment) & (key_row <= row)
        s = jnp.where(allowed, dot_t(q, rk), NEG)
        m = jnp.max(s, axis=1, keepdims=True)
        p = jnp.where(allowed, jnp.exp2((s - m) * c1), 0.0)
        parts.append((m, jnp.sum(p, axis=1, keepdims=True), dot(p.astype(BF16), rv)))
        top = jnp.maximum(jnp.maximum(parts[0][0], parts[1][0]), parts[2][0])
        total = jnp.zeros((CHUNK, LANES), F32)
        acc = jnp.zeros((CHUNK, HD), F32)
        for m, t, a in parts:
            w = jnp.exp2((m - top) * c1)
            total = total + w * t
            acc = acc + w * a
        acc_s[chunk * tiles : (chunk + 1) * tiles] = acc.astype(BF16).reshape(tiles, 16, HD)
        here = lane == (me % 8) * 16 + n % 16
        for which, stat in ((0, top), (1, total)):
            packed = jnp.where(here, stat, 0.0).reshape(tiles, 16, LANES)
            st_s[chunk * tiles : (chunk + 1) * tiles, which : which + 1, :] = jnp.sum(
                packed, axis=1, keepdims=True
            )

    for chunk in range(qrows // CHUNK):
        attend(chunk)

    for k in range(1, plane):
        peer = ((ctx + 2 * k) % nctx, y)
        to = (me + k) % plane
        send(8, st_s.at[to], st_r.at[me], peer)
        send(9, acc_s.at[to], acc_r.at[me], peer)
    acc_r[me] = acc_s[me]
    st_r[me] = st_s[me]

    bytes_of(5, resbuf.at[1]).wait_recv()
    at = pl.multiple_of(y * 16, 16)
    around = jnp.concatenate(
        [resbuf[0, pl.ds(at, 16), :], resbuf[1, pl.ds(at, 16), :]], axis=0
    ).astype(F32)
    into = iota((16, 32), 0)
    inner = into % 8
    source = (into // 8) * 16 + 4 * (inner // 2) + 2 * core + inner % 2
    pick = jnp.where(iota((16, 32), 1) == source, 1.0, 0.0)
    residual = dot(pick.astype(BF16), around.astype(BF16))
    upper = iota((16, LANES), 0) < 8
    gain = jnp.where(upper, own[0:1], other[0:1])

    bytes_of(8, st_r.at[0 : plane - 1]).wait_recv()
    bytes_of(9, acc_r.at[0 : plane - 1]).wait_recv()

    stats = [jnp.sum(st_r[x * 8 : (x + 1) * 8], axis=0) for x in range(plane // 8)]
    m = jnp.concatenate([s[0:1] for s in stats], axis=0)
    total = jnp.concatenate([s[1:2] for s in stats], axis=0)

    def around_lanes(x, join):
        for shift in (16, 32, 64):
            x = join(x, pltpu.roll(x, shift, 1))
        return x

    top = around_lanes(jnp.max(m, axis=0, keepdims=True), jnp.maximum)
    w = jnp.exp2((m - top) * c1)
    total = around_lanes(jnp.sum(w * total, axis=0, keepdims=True), jnp.add)
    w = w / total
    diagonal = iota((16, LANES), 1) % 16 == iota((16, LANES), 0)
    w = jnp.concatenate(
        [jnp.where(diagonal, w[x : x + 1], 0.0) for x in range(plane // 8)], axis=1
    )
    high = w.astype(BF16)
    low = (w - high.astype(F32)).astype(BF16)
    partials = acc_r[...].reshape(qrows, HD)
    attention = dot(high, partials) + dot(low, partials)
    abuf[me] = attention.astype(BF16)
    for peer in plane_peers():
        send(10, abuf.at[me], abuf.at[me], peer)
    bytes_of(6, wbuf.at[1]).wait_recv()
    bytes_of(7, vwbuf.at[0:LANES]).wait_recv()
    bytes_of(4, tbuf.at[0 : plane - 1]).wait_recv()
    target = jnp.concatenate([tbuf[j] for j in range(plane)], axis=0).reshape(groups, 8, LANES)
    bytes_of(10, abuf.at[0 : plane - 1]).wait_recv()

    heads = dot(perm[...], abuf[...].reshape(qrows, HD)).astype(BF16)
    heads = jnp.concatenate([heads[h * rows : (h + 1) * rows] for h in range(HEADS)], axis=1)
    terms = [dot(heads, wbuf[half]).reshape(ny, 8, LANES) for half in range(2)]
    t_s[...] = jnp.concatenate(terms, axis=1).astype(BF16)
    for k in range(1, ny):
        to = (y + k) % ny
        send(11, t_s.at[to], t_r.at[y], (ctx, to))
    t_r[y] = t_s[y]
    bytes_of(11, t_r.at[0 : ny - 1]).wait_recv()
    mixed = jnp.sum(t_r[...].astype(F32), axis=0)
    hidden = residual + mixed
    hbuf[y] = (hidden * gain).astype(BF16)
    for peer in y_peers():
        send(12, hbuf.at[y], hbuf.at[y], peer)
    bytes_of(12, hbuf.at[0 : ny - 1]).wait_recv()

    gathered = hbuf[...].astype(F32)
    halves = [gathered[:, :8], gathered[:, 8:]]
    plain = [halves[0] / own[0:1], halves[1] / other[0:1]]
    squares = jnp.sum(plain[0] * plain[0] + plain[1] * plain[1], axis=2, keepdims=True)
    x = jnp.concatenate(halves, axis=2)

    span = width // 4
    blocks = span // LANES
    logits = []
    picked = jnp.zeros((groups, 8, 1), F32)
    for q in range(4):
        turned = roll_rows(x, 2 * q, 8).reshape(rows, 2 * LANES).astype(BF16)
        part = dot(turned, vwbuf[:, q * span : (q + 1) * span]).reshape(groups, 8, span)
        column = y * width + q * span + iota((groups, 8, span), 2)
        wanted = roll_rows(target, 2 * q, 8)[:, :, 0:1]
        found = jnp.sum(jnp.where(column == wanted, part, 0.0), axis=2, keepdims=True)
        picked = picked + roll_rows(found, -2 * q, 8)
        logits.append(part)
    pair = iota((groups, 8, LANES), 1) // 2
    for u in range(4):
        pieces = []
        for b in range(blocks):
            cut = [part[:, :, b * LANES : (b + 1) * LANES] for part in logits]
            piece = cut[(u - 3) % 4]
            for p in range(3):
                piece = jnp.where(pair == p, cut[(u - p) % 4], piece)
            pieces.append(piece)
        l_s[:, u] = jnp.concatenate(pieces, axis=1).astype(BF16)
    own_group, own_place = me // 4, me % 4
    for k in range(1, plane):
        peer = ((ctx + 2 * k) % nctx, y)
        to = (me + k) % plane
        send(13, l_s.at[to // 4, to % 4], l_r.at[me], peer)
    l_r[me] = l_s[own_group, own_place]
    both = jnp.where(iota((groups, 8, LANES), 2) < 64, squares, picked)
    for j in range(plane):
        s2_s[j] = both[j // 4, 2 * (j % 4) : 2 * (j % 4) + 2]
    for k in range(1, plane):
        peer = ((ctx + 2 * k) % nctx, y)
        send(14, s2_s.at[(me + k) % plane], s2_r.at[me], peer)
    s2_r[me] = s2_s[me]
    bytes_of(13, l_r.at[0 : plane - 1]).wait_recv()
    bytes_of(14, s2_r.at[0 : plane - 1]).wait_recv()

    total = jnp.sum(l_r[...].astype(F32), axis=0)
    both = jnp.sum(s2_r[...], axis=0)
    both = jnp.concatenate([both] * 4, axis=0)
    inverse = lax.rsqrt(both[:, 0:1] / features + EPS)
    picked = both[:, 64:65] * inverse
    logit = total.reshape(-1, 8, LANES) * inverse

    def around_pairs(x, join):
        x = jnp.broadcast_to(x, (8, LANES))
        for shift in (2, 4):
            x = join(x, pltpu.roll(x, shift, 0))
        return x

    top = around_pairs(jnp.max(jnp.max(logit, axis=0), axis=1, keepdims=True), jnp.maximum)
    sums = jnp.sum(jnp.sum(jnp.exp(logit - top), axis=0), axis=1, keepdims=True)
    sums = around_pairs(sums, jnp.add)
    lane8 = iota((8, LANES), 1)
    f_r[y] = jnp.where(lane8 < 32, top, jnp.where(lane8 < 64, sums, picked))
    for peer in y_peers():
        send(15, f_r.at[y], f_r.at[y], peer)
    bytes_of(15, f_r.at[0 : ny - 1]).wait_recv()
    final = f_r[...]
    tops = final[:, :, 0:1]
    top = jnp.max(tops, axis=0)
    sums = jnp.sum(final[:, :, 32:33] * jnp.exp(tops - top), axis=0)
    lse = top + jnp.log(sums)
    picked = jnp.sum(final[:, :, 64:65], axis=0)
    out_ref[...] = jnp.where(lane8 < 64, lse, picked)

    bytes_of(0, qbuf.at[0 : plane - 1]).wait_send()
    bytes_of(1, misc.at[1]).wait_send()
    bytes_of(2, kbuf.at[1]).wait_send()
    bytes_of(3, vbuf.at[1]).wait_send()
    bytes_of(4, tbuf.at[0 : plane - 1]).wait_send()
    bytes_of(5, resbuf.at[1]).wait_send()
    bytes_of(6, wbuf.at[1]).wait_send()
    bytes_of(7, vwbuf.at[0:LANES]).wait_send()
    bytes_of(8, st_r.at[0 : plane - 1]).wait_send()
    bytes_of(9, acc_r.at[0 : plane - 1]).wait_send()
    bytes_of(10, abuf.at[0 : plane - 1]).wait_send()
    bytes_of(11, t_r.at[0 : ny - 1]).wait_send()
    bytes_of(12, hbuf.at[0 : ny - 1]).wait_send()
    bytes_of(13, l_r.at[0 : plane - 1]).wait_send()
    bytes_of(14, s2_r.at[0 : plane - 1]).wait_send()
    bytes_of(15, f_r.at[0 : ny - 1]).wait_send()


def body(plane, ny, *args):
    (
        queries,
        cache_keys,
        cache_values,
        reply_keys,
        reply_values,
        block_prompt,
        lengths,
        residual,
        norm_gain,
        out_weight,
        vocab_weight,
        targets,
    ) = args
    width = vocab_weight.shape[1]
    keys = cache_keys.shape[0]
    rows = 2 * plane
    qrows = 16 * plane
    anywhere = pl.BlockSpec(memory_space=pl.ANY)
    smem = pl.BlockSpec(memory_space=pltpu.SMEM)
    vmem = pltpu.VMEM
    out = pl.pallas_call(
        functools.partial(kernel, plane, ny, width),
        out_shape=jax.ShapeDtypeStruct((8, LANES), F32),
        in_specs=[
            anywhere,
            anywhere,
            anywhere,
            anywhere,
            anywhere,
            smem,
            smem,
            anywhere,
            anywhere,
            anywhere,
            anywhere,
            smem,
        ],
        out_specs=pl.BlockSpec(memory_space=pltpu.VMEM),
        scratch_shapes=[
            vmem(queries.shape, BF16),
            vmem(reply_keys.shape, BF16),
            vmem(reply_values.shape, BF16),
            vmem((1, LANES), F32),
            vmem((2, keys, HD), BF16),
            vmem((2, keys, HD), BF16),
            vmem((2,) + residual.shape, BF16),
            vmem((2,) + out_weight.shape, BF16),
            vmem((2 * LANES, width), BF16),
            vmem((2, 8, LANES), F32),
            vmem((plane, 16, HD), BF16),
            vmem((2, LANES), jnp.int32),
            vmem((plane, 2, LANES), jnp.int32),
            vmem((qrows, qrows), BF16),
            vmem((plane, 16, HD), BF16),
            vmem((plane, 16, HD), BF16),
            vmem((plane, 2, LANES), F32),
            vmem((plane, 2, LANES), F32),
            vmem((plane, 16, HD), BF16),
            vmem((ny, 16, LANES), BF16),
            vmem((ny, 16, LANES), BF16),
            vmem((ny, 16, LANES), BF16),
            vmem((plane // 4, 4, 2 * width // LANES, LANES), BF16),
            vmem((plane, 2 * width // LANES, LANES), BF16),
            vmem((plane, 2, LANES), F32),
            vmem((plane, 2, LANES), F32),
            vmem((ny, 8, LANES), F32),
            pltpu.SemaphoreType.DMA((9,)),
            pltpu.SemaphoreType.DMA((16,)),
            pltpu.SemaphoreType.DMA((16,)),
        ],
        compiler_params=pltpu.CompilerParams(
            collective_id=0, has_side_effects=True, vmem_limit_bytes=40 * 2**20
        ),
    )(
        queries,
        cache_keys,
        cache_values,
        reply_keys,
        reply_values,
        block_prompt,
        lengths,
        residual,
        norm_gain.reshape(1, LANES),
        out_weight,
        vocab_weight,
        targets,
    )
    return out[0:2, 0], out[0:2, 64]


def solution(mesh):
    plane, ny = mesh.shape["ctx"] // 2, mesh.shape["tp"]
    return jax.shard_map(
        functools.partial(body, plane, ny),
        mesh=mesh,
        in_specs=(
            P("ctx", "tp"),
            P("ctx", "tp"),
            P("ctx", "tp"),
            P("ctx", "tp"),
            P("ctx", "tp"),
            P("ctx"),
            P(),
            P(None, "ctx"),
            P("ctx"),
            P("tp", "ctx"),
            P("ctx", "tp"),
            P("ctx"),
        ),
        out_specs=(P("ctx"), P("ctx")),
        check_vma=False,
    )
```

```python
import functools

import jax
import jax.numpy as jnp
from jax import lax
from jax.experimental import pallas as pl
from jax.experimental.pallas import tpu as pltpu
from jax.sharding import PartitionSpec as P

MESH = pl.DeviceIdType.MESH
F32 = jnp.float32
BF16 = jnp.bfloat16

HD = 128
HEADS = 8
NEG = -1e30
EPS = 1e-06
LOG2E = 1.4426950408889634
LANES = 128
CHUNK = 128


def iota(shape, dim):
    return lax.broadcasted_iota(jnp.int32, shape, dim)


def dot(a, b):
    return jnp.dot(a, b, preferred_element_type=F32)


def dot_t(a, b):
    return lax.dot_general(a, b, (((1,), (1,)), ((), ())), preferred_element_type=F32)


def roll_rows(x, shift):
    shift = shift % 8
    return jnp.concatenate([x[shift:], x[:shift]], axis=0) if shift else x


def kernel(
    plane,
    ny,
    width,
    q_hbm,
    k_hbm,
    v_hbm,
    rk_hbm,
    rv_hbm,
    bp_hbm,
    len_hbm,
    res_hbm,
    gain_hbm,
    w_hbm,
    vw_hbm,
    tgt_hbm,
    out_ref,
    q_in,
    rk_in,
    rv_in,
    gain_in,
    bp_smem,
    len_smem,
    tgt_smem,
    kbuf,
    vbuf,
    resbuf,
    wbuf,
    vwbuf,
    misc,
    qbuf,
    tsrc,
    tbuf,
    acc_s,
    acc_r,
    st_s,
    st_r,
    abuf,
    t_s,
    t_r,
    hbuf,
    l_s,
    l_r,
    s2_s,
    s2_r,
    f_r,
    local_sem,
    send_sem,
    recv_sem,
):
    ctx = lax.axis_index("ctx")
    y = lax.axis_index("tp")
    core = ctx % 2
    me = ctx // 2
    partner = (ctx + 1 - 2 * core, y)
    nctx = 2 * plane
    qrows = 16 * plane
    features = nctx * LANES
    c1 = (HD ** (-0.5)) * LOG2E

    nz = 8
    nx = plane // nz
    along_x = [((me // nz + dx) % nx) * nz for dx in range(nx)]
    along_z = [(me % nz + dz) % nz for dz in range(nz)]
    steps = [(dx, dz) for dx in range(nx) for dz in range(nz) if dx or dz]
    steps.sort(key=lambda s: -min(s[0], nx - s[0]) - min(s[1], nz - s[1]))
    plane_to = [along_x[dx] + along_z[dz] for dx, dz in steps]
    plane_peers = [(to, (2 * to + core, y)) for to in plane_to]
    y_steps = sorted(range(1, ny), key=lambda s: -min(s, ny - s))
    y_peers = [((y + k) % ny, (ctx, (y + k) % ny)) for k in y_steps]

    barrier = pltpu.get_barrier_semaphore()
    greeted = [device for _, device in plane_peers + y_peers] + [partner]
    for peer in greeted:
        pl.semaphore_signal(barrier, inc=1, device_id=peer, device_id_type=MESH)

    def local(index, src, dst):
        copy = pltpu.make_async_copy(src, dst, local_sem.at[index])
        copy.start()
        return copy

    copies = [
        local(0, q_hbm, q_in),
        local(1, rk_hbm, rk_in),
        local(2, rv_hbm, rv_in),
        local(3, gain_hbm, gain_in),
        local(9, bp_hbm, bp_smem),
        local(10, len_hbm, len_smem),
        local(11, tgt_hbm, tgt_smem),
    ]
    big = [
        local(4, k_hbm, kbuf.at[0]),
        local(5, v_hbm, vbuf.at[0]),
        local(6, res_hbm, resbuf.at[0]),
        local(7, w_hbm, wbuf.at[0]),
        local(8, vw_hbm, vwbuf.at[0:LANES]),
    ]
    for copy in copies:
        copy.wait()

    def send(index, src, dst, peer):
        pltpu.make_async_remote_copy(
            src_ref=src,
            dst_ref=dst,
            send_sem=send_sem.at[index],
            recv_sem=recv_sem.at[index],
            device_id=peer,
            device_id_type=MESH,
        ).start()

    def bytes_of(index, ref):
        return pltpu.make_async_remote_copy(
            src_ref=ref,
            dst_ref=ref,
            send_sem=send_sem.at[index],
            recv_sem=recv_sem.at[index],
            device_id=partner,
            device_id_type=MESH,
        )

    qf = q_in[...].astype(F32)
    tile = jnp.concatenate([qf[:, h * HD : (h + 1) * HD] for h in range(HEADS)], axis=0)
    qbuf[me] = tile.astype(BF16)
    misc[0, 0:1, :] = gain_in[...]
    misc[0, 1:2, :] = jnp.full((1, LANES), bp_smem[0], jnp.int32).astype(F32)
    misc[0, 2:4, :] = rk_in[...].astype(F32)
    misc[0, 4:6, :] = rv_in[...].astype(F32)
    misc[0, 6:8, :] = jnp.zeros((2, LANES), F32)
    two = iota((2, LANES), 0)
    tsrc[...] = jnp.where(two == 0, tgt_smem[0], tgt_smem[1])
    tbuf[me] = tsrc[...]

    pl.semaphore_wait(barrier, len(greeted))

    for (dx, _), (_, peer) in zip(steps, plane_peers):
        send(16 + dx, qbuf.at[me], qbuf.at[me], peer)
    send(1, misc.at[0], misc.at[1], partner)
    send(2, k_hbm, kbuf.at[1], partner)
    send(3, v_hbm, vbuf.at[1], partner)
    send(5, res_hbm, resbuf.at[1], partner)
    send(6, w_hbm, wbuf.at[1], partner)
    send(7, vw_hbm, vwbuf.at[LANES : 2 * LANES], partner)

    into = iota((nz * 16, nz * 16), 0)
    source = (into // 2 % nz) * 16 + (into // (2 * nz)) * 2 + into % 2
    perm = jnp.where(iota((nz * 16, nz * 16), 1) == source, 1.0, 0.0).astype(BF16)

    end0 = len_smem[0]
    end1 = end0 + len_smem[1]
    end2 = end1 + len_smem[2]

    def segment(index):
        one = lambda end: jnp.where(index >= end, 1, 0)
        return one(end0) + one(end1) + one(end2) + one(end2 + len_smem[3])

    for copy in big:
        copy.wait()
    bytes_of(1, misc.at[1]).wait_recv()
    bytes_of(2, kbuf.at[1]).wait_recv()
    bytes_of(3, vbuf.at[1]).wait_recv()

    own, other = misc[0], misc[1]
    fill = jnp.zeros((LANES - 4, HD), F32)
    rk = jnp.concatenate([own[2:4], other[2:4], fill], axis=0).astype(BF16)
    rv = jnp.concatenate([own[4:6], other[4:6], fill], axis=0).astype(BF16)
    prompts = (own[1:2, 0:1], other[1:2, 0:1])
    lane = iota((CHUNK, LANES), 1)
    key_row = jnp.where(lane < 2, 2 * ctx + lane, 2 * (ctx + 1 - 2 * core) + lane - 2)
    key_segment = segment(key_row)

    tiles = CHUNK // 16

    def attend(at):
        first = at * 16
        q = qbuf[pl.ds(at, tiles)].reshape(CHUNK, HD)
        n = first + iota((CHUNK, LANES), 0)
        row = 4 * (n // 16) + 2 * core + n % 2
        row_segment = segment(row)
        row_prompt = (row_segment // 2).astype(F32)
        parts = []
        for block in range(2):
            s = dot_t(q, kbuf[block])
            m = jnp.max(s, axis=1, keepdims=True)
            p = jnp.exp2((s - m) * c1)
            total = jnp.sum(p, axis=1, keepdims=True)
            acc = dot(p.astype(BF16), vbuf[block])
            m = jnp.where(row_prompt == prompts[block], m, NEG)
            parts.append((m, total, acc))
        allowed = (lane < 4) & (key_segment == row_segment) & (key_row <= row)
        s = jnp.where(allowed, dot_t(q, rk), NEG)
        m = jnp.max(s, axis=1, keepdims=True)
        p = jnp.where(allowed, jnp.exp2((s - m) * c1), 0.0)
        parts.append((m, jnp.sum(p, axis=1, keepdims=True), dot(p.astype(BF16), rv)))
        top = jnp.maximum(jnp.maximum(parts[0][0], parts[1][0]), parts[2][0])
        total = jnp.zeros((CHUNK, LANES), F32)
        acc = jnp.zeros((CHUNK, HD), F32)
        for m, t, a in parts:
            w = jnp.exp2((m - top) * c1)
            total = total + w * t
            acc = acc + w * a
        acc_s[pl.ds(at, tiles)] = acc.astype(BF16).reshape(tiles, 16, HD)
        here = lane == (me % 8) * 16 + n % 16
        for which, stat in ((0, top), (1, total)):
            packed = jnp.where(here, stat, 0.0).reshape(tiles, 16, LANES)
            st_s[pl.ds(at, tiles), which : which + 1, :] = jnp.sum(
                packed, axis=1, keepdims=True
            )

    for dx in sorted(range(nx), key=lambda d: min(d, nx - d) if d != nx - 1 else nx):
        bytes_of(16 + dx, qbuf.at[0 : nz - (dx == 0)]).wait_recv()
        attend(along_x[(nx - dx) % nx])
        for (back, _), (to, peer) in zip(steps, plane_peers):
            if back == (nx - dx) % nx:
                send(8, st_s.at[to], st_r.at[me], peer)
                send(9, acc_s.at[to], acc_r.at[me], peer)
    acc_r[me] = acc_s[me]
    st_r[me] = st_s[me]

    bytes_of(5, resbuf.at[1]).wait_recv()
    at = pl.multiple_of(y * 16, 16)
    around = jnp.concatenate(
        [resbuf[0, pl.ds(at, 16), :], resbuf[1, pl.ds(at, 16), :]], axis=0
    ).astype(F32)
    into = iota((16, 32), 0)
    inner = into % 8
    source = (into // 8) * 16 + 4 * (inner // 2) + 2 * core + inner % 2
    pick = jnp.where(iota((16, 32), 1) == source, 1.0, 0.0)
    residual = dot(pick.astype(BF16), around.astype(BF16))
    upper = iota((16, LANES), 0) < 8
    gain = jnp.where(upper, own[0:1], other[0:1])

    bytes_of(8, st_r.at[0 : plane - 1]).wait_recv()
    bytes_of(9, acc_r.at[0 : plane - 1]).wait_recv()

    stats = [jnp.sum(st_r[x * 8 : (x + 1) * 8], axis=0) for x in range(plane // 8)]
    m = jnp.concatenate([s[0:1] for s in stats], axis=0)
    total = jnp.concatenate([s[1:2] for s in stats], axis=0)

    def around_lanes(x, join):
        for shift in (16, 32, 64):
            x = join(x, pltpu.roll(x, shift, 1))
        return x

    top = around_lanes(jnp.max(m, axis=0, keepdims=True), jnp.maximum)
    w = jnp.exp2((m - top) * c1)
    total = around_lanes(jnp.sum(w * total, axis=0, keepdims=True), jnp.add)
    w = w / total
    diagonal = iota((16, LANES), 1) % 16 == iota((16, LANES), 0)
    w = jnp.concatenate(
        [jnp.where(diagonal, w[x : x + 1], 0.0) for x in range(plane // 8)], axis=1
    )
    high = w.astype(BF16)
    low = (w - high.astype(F32)).astype(BF16)
    partials = acc_r[...].reshape(qrows, HD)
    attention = dot(high, partials) + dot(low, partials)
    abuf[me] = attention.astype(BF16)
    for (dx, _), (_, peer) in zip(steps, plane_peers):
        send(4 if dx == 0 else 27 + dx, abuf.at[me], abuf.at[me], peer)
    for _, peer in plane_peers:
        send(0, tsrc, tbuf.at[me], peer)
    bytes_of(6, wbuf.at[1]).wait_recv()
    bytes_of(7, vwbuf.at[0:LANES]).wait_recv()

    share = ny // nx
    for dx in sorted(range(nx), key=lambda d: min(d, nx - d)):
        bytes_of(4 if dx == 0 else 27 + dx, abuf.at[0 : nz - (dx == 0)]).wait_recv()
        at = along_x[(nx - dx) % nx]
        heads = dot(perm, abuf[pl.ds(at, nz)].reshape(nz * 16, HD)).astype(BF16)
        span = 2 * nz
        heads = jnp.concatenate([heads[h * span : (h + 1) * span] for h in range(HEADS)], axis=1)
        terms = [dot(heads, wbuf[half]).reshape(share, 8, LANES) for half in range(2)]
        to = at // nz * share
        t_s[pl.ds(to, share)] = jnp.concatenate(terms, axis=1).astype(BF16)
        for k in range(share):
            pl.when(to + k != y)(
                lambda to=to + k: send(11, t_s.at[to], t_r.at[y], (ctx, to))
            )
    t_r[y] = t_s[y]
    bytes_of(11, t_r.at[0 : ny - 1]).wait_recv()
    mixed = jnp.sum(t_r[...].astype(F32), axis=0)
    hidden = residual + mixed
    hbuf[y] = (hidden * gain).astype(BF16)
    for k, (_, peer) in zip(y_steps, y_peers):
        send(19 + k, hbuf.at[y], hbuf.at[y], peer)
    bytes_of(0, tbuf.at[0 : plane - 1]).wait_recv()

    span = width // 4
    blocks = span // LANES
    pair = iota((8, LANES), 0) // 2
    for dy in sorted(range(ny), key=lambda d: min(d, ny - d)):
        if dy:
            bytes_of(19 + dy, hbuf.at[0]).wait_recv()
        group = (y + ny - dy) % ny
        gathered = hbuf[group].astype(F32)
        halves = [gathered[:8], gathered[8:]]
        plain = [halves[0] / own[0:1], halves[1] / other[0:1]]
        squares = jnp.sum(plain[0] * plain[0] + plain[1] * plain[1], axis=1, keepdims=True)
        x = jnp.concatenate(halves, axis=1)
        turned = jnp.concatenate([roll_rows(x, 2 * q) for q in range(4)], axis=0).astype(BF16)
        product = dot(turned, vwbuf[...])
        marks = tbuf[pl.ds(group * 4, 4)]
        target = jnp.concatenate([marks[u] for u in range(4)], axis=0)
        logits = []
        picked = jnp.zeros((8, 1), F32)
        for q in range(4):
            part = product[8 * q : 8 * q + 8, q * span : (q + 1) * span]
            column = y * width + q * span + iota((8, span), 1)
            wanted = roll_rows(target, 2 * q)[:, 0:1]
            found = jnp.sum(jnp.where(column == wanted, part, 0.0), axis=1, keepdims=True)
            picked = picked + roll_rows(found, -2 * q)
            logits.append(part)
        both = jnp.where(iota((8, LANES), 1) < 64, squares, picked)
        for u in range(4):
            pieces = []
            for b in range(blocks):
                cut = [part[:, b * LANES : (b + 1) * LANES] for part in logits]
                piece = cut[(u - 3) % 4]
                for p in range(3):
                    piece = jnp.where(pair == p, cut[(u - p) % 4], piece)
                pieces.append(piece)
            l_s[group, u] = jnp.concatenate(pieces, axis=0).astype(BF16)
            to = group * 4 + u
            s2_s[to] = both[2 * u : 2 * u + 2]

            @pl.when(to != me)
            def _(u=u, to=to, group=group):
                peer = (2 * to + core, y)
                send(13, l_s.at[group, u], l_r.at[me], peer)
                send(14, s2_s.at[to], s2_r.at[me], peer)

    l_r[me] = l_s[me // 4, me % 4]
    s2_r[me] = s2_s[me]
    bytes_of(13, l_r.at[0 : plane - 1]).wait_recv()
    bytes_of(14, s2_r.at[0 : plane - 1]).wait_recv()

    total = jnp.sum(l_r[...].astype(F32), axis=0)
    both = jnp.sum(s2_r[...], axis=0)
    both = jnp.concatenate([both] * 4, axis=0)
    inverse = lax.rsqrt(both[:, 0:1] / features + EPS)
    picked = both[:, 64:65] * inverse
    logit = total.reshape(-1, 8, LANES) * inverse

    def around_pairs(x, join):
        x = jnp.broadcast_to(x, (8, LANES))
        for shift in (2, 4):
            x = join(x, pltpu.roll(x, shift, 0))
        return x

    top = around_pairs(jnp.max(jnp.max(logit, axis=0), axis=1, keepdims=True), jnp.maximum)
    sums = jnp.sum(jnp.sum(jnp.exp(logit - top), axis=0), axis=1, keepdims=True)
    sums = around_pairs(sums, jnp.add)
    lane8 = iota((8, LANES), 1)
    f_r[y] = jnp.where(lane8 < 32, top, jnp.where(lane8 < 64, sums, picked))
    for _, peer in y_peers:
        send(15, f_r.at[y], f_r.at[y], peer)
    bytes_of(15, f_r.at[0 : ny - 1]).wait_recv()
    final = f_r[...]
    tops = final[:, :, 0:1]
    top = jnp.max(tops, axis=0)
    sums = jnp.sum(final[:, :, 32:33] * jnp.exp(tops - top), axis=0)
    lse = top + jnp.log(sums)
    picked = jnp.sum(final[:, :, 64:65], axis=0)
    out_ref[...] = jnp.where(lane8 < 64, lse, picked)

    for dx in range(nx):
        bytes_of(16 + dx, qbuf.at[0 : nz - (dx == 0)]).wait_send()
        bytes_of(4 if dx == 0 else 27 + dx, abuf.at[0 : nz - (dx == 0)]).wait_send()
    for k in range(1, ny):
        bytes_of(19 + k, hbuf.at[0]).wait_send()
    bytes_of(1, misc.at[1]).wait_send()
    bytes_of(2, kbuf.at[1]).wait_send()
    bytes_of(3, vbuf.at[1]).wait_send()
    bytes_of(0, tbuf.at[0 : plane - 1]).wait_send()
    bytes_of(5, resbuf.at[1]).wait_send()
    bytes_of(6, wbuf.at[1]).wait_send()
    bytes_of(7, vwbuf.at[0:LANES]).wait_send()
    bytes_of(8, st_r.at[0 : plane - 1]).wait_send()
    bytes_of(9, acc_r.at[0 : plane - 1]).wait_send()
    bytes_of(11, t_r.at[0 : ny - 1]).wait_send()
    bytes_of(13, l_r.at[0 : plane - 1]).wait_send()
    bytes_of(14, s2_r.at[0 : plane - 1]).wait_send()
    bytes_of(15, f_r.at[0 : ny - 1]).wait_send()


def body(plane, ny, *args):
    (
        queries,
        cache_keys,
        cache_values,
        reply_keys,
        reply_values,
        block_prompt,
        lengths,
        residual,
        norm_gain,
        out_weight,
        vocab_weight,
        targets,
    ) = args
    width = vocab_weight.shape[1]
    keys = cache_keys.shape[0]
    hbm = pl.BlockSpec(memory_space=pltpu.HBM)
    vmem = pltpu.VMEM
    out = pl.pallas_call(
        functools.partial(kernel, plane, ny, width),
        out_shape=jax.ShapeDtypeStruct((8, LANES), F32),
        in_specs=[hbm] * len(args),
        out_specs=pl.BlockSpec(memory_space=pltpu.VMEM),
        scratch_shapes=[
            vmem(queries.shape, BF16),
            vmem(reply_keys.shape, BF16),
            vmem(reply_values.shape, BF16),
            vmem((1, LANES), F32),
            pltpu.SMEM(block_prompt.shape, jnp.int32),
            pltpu.SMEM(lengths.shape, jnp.int32),
            pltpu.SMEM(targets.shape, jnp.int32),
            vmem((2, keys, HD), BF16),
            vmem((2, keys, HD), BF16),
            vmem((2,) + residual.shape, BF16),
            vmem((2,) + out_weight.shape, BF16),
            vmem((2 * LANES, width), BF16),
            vmem((2, 8, LANES), F32),
            vmem((plane, 16, HD), BF16),
            vmem((2, LANES), jnp.int32),
            vmem((plane, 2, LANES), jnp.int32),
            vmem((plane, 16, HD), BF16),
            vmem((plane, 16, HD), BF16),
            vmem((plane, 2, LANES), F32),
            vmem((plane, 2, LANES), F32),
            vmem((plane, 16, HD), BF16),
            vmem((ny, 16, LANES), BF16),
            vmem((ny, 16, LANES), BF16),
            vmem((ny, 16, LANES), BF16),
            vmem((plane // 4, 4, 2 * width // LANES, LANES), BF16),
            vmem((plane, 2 * width // LANES, LANES), BF16),
            vmem((plane, 2, LANES), F32),
            vmem((plane, 2, LANES), F32),
            vmem((ny, 8, LANES), F32),
            pltpu.SemaphoreType.DMA((12,)),
            pltpu.SemaphoreType.DMA((32,)),
            pltpu.SemaphoreType.DMA((32,)),
        ],
        compiler_params=pltpu.CompilerParams(
            collective_id=0, has_side_effects=True, vmem_limit_bytes=60 * 2**20
        ),
    )(
        queries,
        cache_keys,
        cache_values,
        reply_keys,
        reply_values,
        block_prompt,
        lengths,
        residual,
        norm_gain.reshape(1, LANES),
        out_weight,
        vocab_weight,
        targets,
    )
    return out[0:2, 0], out[0:2, 64]


def solution(mesh):
    plane, ny = mesh.shape["ctx"] // 2, mesh.shape["tp"]
    return jax.shard_map(
        functools.partial(body, plane, ny),
        mesh=mesh,
        in_specs=(
            P("ctx", "tp"),
            P("ctx", "tp"),
            P("ctx", "tp"),
            P("ctx", "tp"),
            P("ctx", "tp"),
            P("ctx"),
            P(),
            P(None, "ctx"),
            P("ctx"),
            P("tp", "ctx"),
            P("ctx", "tp"),
            P("ctx"),
        ),
        out_specs=(P("ctx"), P("ctx")),
        check_vma=False,
    )
```

```python
import functools

import jax
import jax.numpy as jnp
from jax import lax
from jax.experimental import pallas as pl
from jax.experimental.pallas import tpu as pltpu
from jax.sharding import PartitionSpec as P

MESH = pl.DeviceIdType.MESH
F32 = jnp.float32
BF16 = jnp.bfloat16

HD = 128
HEADS = 8
NEG = -1e30
EPS = 1e-06
LOG2E = 1.4426950408889634
LANES = 128
CHUNK = 128


def iota(shape, dim):
    return lax.broadcasted_iota(jnp.int32, shape, dim)


def dot(a, b):
    return jnp.dot(a, b, preferred_element_type=F32)


def dot_t(a, b):
    return lax.dot_general(a, b, (((1,), (1,)), ((), ())), preferred_element_type=F32)


def roll_rows(x, shift):
    shift = shift % 8
    return jnp.concatenate([x[shift:], x[:shift]], axis=0) if shift else x


def kernel(
    plane,
    ny,
    width,
    q_hbm,
    k_hbm,
    v_hbm,
    rk_hbm,
    rv_hbm,
    bp_hbm,
    len_hbm,
    res_hbm,
    gain_hbm,
    w_hbm,
    vw_hbm,
    tgt_hbm,
    out_ref,
    q_in,
    rk_in,
    rv_in,
    gain_in,
    bp_smem,
    len_smem,
    tgt_smem,
    kbuf,
    vbuf,
    resbuf,
    wbuf,
    vwbuf,
    misc,
    qbuf,
    tsrc,
    tbuf,
    acc_s,
    acc_r,
    st_s,
    st_r,
    abuf,
    t_s,
    t_r,
    hbuf,
    l_s,
    l_r,
    s2_s,
    s2_r,
    f_r,
    local_sem,
    send_sem,
    recv_sem,
):
    ctx = lax.axis_index("ctx")
    y = lax.axis_index("tp")
    core = ctx % 2
    me = ctx // 2
    partner = (ctx + 1 - 2 * core, y)
    nctx = 2 * plane
    qrows = 16 * plane
    features = nctx * LANES
    c1 = (HD ** (-0.5)) * LOG2E

    nz = 8
    nx = plane // nz
    along_x = [((me // nz + dx) % nx) * nz for dx in range(nx)]
    along_z = [(me % nz + dz) % nz for dz in range(nz)]
    steps = [(dx, dz) for dx in range(nx) for dz in range(nz) if dx or dz]
    steps.sort(key=lambda s: -min(s[0], nx - s[0]) - min(s[1], nz - s[1]))
    plane_to = [along_x[dx] + along_z[dz] for dx, dz in steps]
    plane_peers = [(to, (2 * to + core, y)) for to in plane_to]
    y_steps = sorted(range(1, ny), key=lambda s: -min(s, ny - s))
    y_peers = [((y + k) % ny, (ctx, (y + k) % ny)) for k in y_steps]

    barrier = pltpu.get_barrier_semaphore()
    greeted = [device for _, device in plane_peers + y_peers] + [partner]
    for peer in greeted:
        pl.semaphore_signal(barrier, inc=1, device_id=peer, device_id_type=MESH)

    def local(index, src, dst):
        copy = pltpu.make_async_copy(src, dst, local_sem.at[index])
        copy.start()
        return copy

    copies = [
        local(0, q_hbm, q_in),
        local(1, rk_hbm, rk_in),
        local(2, rv_hbm, rv_in),
        local(3, gain_hbm, gain_in),
        local(9, bp_hbm, bp_smem),
        local(10, len_hbm, len_smem),
        local(11, tgt_hbm, tgt_smem),
    ]
    big = [
        local(4, k_hbm, kbuf.at[0]),
        local(5, v_hbm, vbuf.at[0]),
        local(6, res_hbm, resbuf.at[0]),
        local(7, w_hbm, wbuf.at[0]),
        local(8, vw_hbm, vwbuf.at[0:LANES]),
    ]
    for copy in copies:
        copy.wait()

    def send(index, src, dst, peer):
        pltpu.make_async_remote_copy(
            src_ref=src,
            dst_ref=dst,
            send_sem=send_sem.at[index],
            recv_sem=recv_sem.at[index],
            device_id=peer,
            device_id_type=MESH,
        ).start()

    def bytes_of(index, ref):
        return pltpu.make_async_remote_copy(
            src_ref=ref,
            dst_ref=ref,
            send_sem=send_sem.at[index],
            recv_sem=recv_sem.at[index],
            device_id=partner,
            device_id_type=MESH,
        )

    qf = q_in[...].astype(F32)
    tile = jnp.concatenate([qf[:, h * HD : (h + 1) * HD] for h in range(HEADS)], axis=0)
    qbuf[me] = tile.astype(BF16)
    misc[0, 0:1, :] = gain_in[...]
    misc[0, 1:2, :] = jnp.full((1, LANES), bp_smem[0], jnp.int32).astype(F32)
    misc[0, 2:4, :] = rk_in[...].astype(F32)
    misc[0, 4:6, :] = rv_in[...].astype(F32)
    misc[0, 6:8, :] = jnp.zeros((2, LANES), F32)
    two = iota((2, LANES), 0)
    tsrc[...] = jnp.where(two == 0, tgt_smem[0], tgt_smem[1])
    tbuf[me] = tsrc[...]

    pl.semaphore_wait(barrier, len(greeted))

    for (dx, _), (_, peer) in zip(steps, plane_peers):
        send(16 + dx, qbuf.at[me], qbuf.at[me], peer)
    send(1, misc.at[0], misc.at[1], partner)
    send(2, k_hbm, kbuf.at[1], partner)
    send(3, v_hbm, vbuf.at[1], partner)
    send(5, res_hbm, resbuf.at[1], partner)
    send(6, w_hbm, wbuf.at[1], partner)
    send(7, vw_hbm, vwbuf.at[LANES : 2 * LANES], partner)

    into = iota((nz * 16, nz * 16), 0)
    source = (into // 2 % nz) * 16 + (into // (2 * nz)) * 2 + into % 2
    perm = jnp.where(iota((nz * 16, nz * 16), 1) == source, 1.0, 0.0).astype(BF16)

    end0 = len_smem[0]
    end1 = end0 + len_smem[1]
    end2 = end1 + len_smem[2]

    def segment(index):
        one = lambda end: jnp.where(index >= end, 1, 0)
        return one(end0) + one(end1) + one(end2) + one(end2 + len_smem[3])

    for copy in big:
        copy.wait()
    bytes_of(1, misc.at[1]).wait_recv()
    bytes_of(2, kbuf.at[1]).wait_recv()
    bytes_of(3, vbuf.at[1]).wait_recv()

    own, other = misc[0], misc[1]
    fill = jnp.zeros((LANES - 4, HD), F32)
    rk = jnp.concatenate([own[2:4], other[2:4], fill], axis=0).astype(BF16)
    rv = jnp.concatenate([own[4:6], other[4:6], fill], axis=0).astype(BF16)
    prompts = (own[1:2, 0:1], other[1:2, 0:1])
    lane = iota((CHUNK, LANES), 1)
    key_row = jnp.where(lane < 2, 2 * ctx + lane, 2 * (ctx + 1 - 2 * core) + lane - 2)
    key_segment = segment(key_row)

    tiles = CHUNK // 16

    def attend(at):
        first = at * 16
        q = qbuf[pl.ds(at, tiles)].reshape(CHUNK, HD)
        n = first + iota((CHUNK, LANES), 0)
        row = 4 * (n // 16) + 2 * core + n % 2
        row_segment = segment(row)
        row_prompt = (row_segment // 2).astype(F32)
        parts = []
        for block in range(2):
            s = dot_t(q, kbuf[block])
            m = jnp.max(s, axis=1, keepdims=True)
            p = jnp.exp2((s - m) * c1)
            total = jnp.sum(p, axis=1, keepdims=True)
            acc = dot(p.astype(BF16), vbuf[block])
            m = jnp.where(row_prompt == prompts[block], m, NEG)
            parts.append((m, total, acc))
        allowed = (lane < 4) & (key_segment == row_segment) & (key_row <= row)
        s = jnp.where(allowed, dot_t(q, rk), NEG)
        m = jnp.max(s, axis=1, keepdims=True)
        p = jnp.where(allowed, jnp.exp2((s - m) * c1), 0.0)
        parts.append((m, jnp.sum(p, axis=1, keepdims=True), dot(p.astype(BF16), rv)))
        top = jnp.maximum(jnp.maximum(parts[0][0], parts[1][0]), parts[2][0])
        total = jnp.zeros((CHUNK, LANES), F32)
        acc = jnp.zeros((CHUNK, HD), F32)
        for m, t, a in parts:
            w = jnp.exp2((m - top) * c1)
            total = total + w * t
            acc = acc + w * a
        acc_s[pl.ds(at, tiles)] = acc.astype(BF16).reshape(tiles, 16, HD)
        here = lane == (me % 8) * 16 + n % 16
        for which, stat in ((0, top), (1, total)):
            packed = jnp.where(here, stat, 0.0).reshape(tiles, 16, LANES)
            st_s[pl.ds(at, tiles), which : which + 1, :] = jnp.sum(
                packed, axis=1, keepdims=True
            )

    for dx in sorted(range(nx), key=lambda d: min(d, nx - d) if d != nx - 1 else nx):
        bytes_of(16 + dx, qbuf.at[0 : nz - (dx == 0)]).wait_recv()
        attend(along_x[(nx - dx) % nx])
        for (back, _), (to, peer) in zip(steps, plane_peers):
            if back == (nx - dx) % nx:
                send(8, st_s.at[to], st_r.at[me], peer)
                send(9, acc_s.at[to], acc_r.at[me], peer)
    acc_r[me] = acc_s[me]
    st_r[me] = st_s[me]

    half = ny // 2
    bytes_of(5, resbuf.at[1]).wait_recv()
    into = iota((16, 32), 0)
    inner = into % 8
    source = (into // 8) * 16 + 4 * (inner // 2) + 2 * core + inner % 2
    pick = jnp.where(iota((16, 32), 1) == source, 1.0, 0.0).astype(BF16)
    residual = []
    for group in (y, (y + half) % ny):
        at = pl.multiple_of(group * 16, 16)
        around = [resbuf[side, pl.ds(at, 16), :] for side in range(2)]
        residual.append(dot(pick, jnp.concatenate(around, axis=0)))
    upper = iota((16, LANES), 0) < 8
    gain = jnp.where(upper, own[0:1], other[0:1])

    bytes_of(8, st_r.at[0 : plane - 1]).wait_recv()
    bytes_of(9, acc_r.at[0 : plane - 1]).wait_recv()

    stats = [jnp.sum(st_r[x * 8 : (x + 1) * 8], axis=0) for x in range(plane // 8)]
    m = jnp.concatenate([s[0:1] for s in stats], axis=0)
    total = jnp.concatenate([s[1:2] for s in stats], axis=0)

    def around_lanes(x, join):
        for shift in (16, 32, 64):
            x = join(x, pltpu.roll(x, shift, 1))
        return x

    top = around_lanes(jnp.max(m, axis=0, keepdims=True), jnp.maximum)
    w = jnp.exp2((m - top) * c1)
    total = around_lanes(jnp.sum(w * total, axis=0, keepdims=True), jnp.add)
    w = w / total
    diagonal = iota((16, LANES), 1) % 16 == iota((16, LANES), 0)
    w = jnp.concatenate(
        [jnp.where(diagonal, w[x : x + 1], 0.0) for x in range(plane // 8)], axis=1
    )
    high = w.astype(BF16)
    low = (w - high.astype(F32)).astype(BF16)
    partials = acc_r[...].reshape(qrows, HD)
    attention = dot(high, partials) + dot(low, partials)
    abuf[me] = attention.astype(BF16)
    for (dx, _), (_, peer) in zip(steps, plane_peers):
        send(4 if dx == 0 else 27 + dx, abuf.at[me], abuf.at[me], peer)
    for _, peer in plane_peers:
        send(0, tsrc, tbuf.at[me], peer)
    bytes_of(6, wbuf.at[1]).wait_recv()
    bytes_of(7, vwbuf.at[0:LANES]).wait_recv()

    share = ny // nx
    for dx in sorted(range(nx), key=lambda d: min(d, nx - d)):
        bytes_of(4 if dx == 0 else 27 + dx, abuf.at[0 : nz - (dx == 0)]).wait_recv()
        at = along_x[(nx - dx) % nx]
        heads = dot(perm, abuf[pl.ds(at, nz)].reshape(nz * 16, HD)).astype(BF16)
        span = 2 * nz
        heads = jnp.concatenate([heads[h * span : (h + 1) * span] for h in range(HEADS)], axis=1)
        terms = [dot(heads, wbuf[half]).reshape(share, 8, LANES) for half in range(2)]
        to = at // nz * share
        t_s[pl.ds(to, share)] = jnp.concatenate(terms, axis=1).astype(BF16)
        for k in range(share):
            for slot in range(2):
                owner = (to + k + slot * half) % ny

                @pl.when(owner != y)
                def _(group=to + k, slot=slot, owner=owner):
                    send(11, t_s.at[group], t_r.at[slot * ny + y], (ctx, owner))

    for slot in range(2):
        t_r[slot * ny + y] = t_s[(y + slot * half) % ny]
    bytes_of(11, t_r.at[0 : 2 * (ny - 1)]).wait_recv()
    for slot in range(2):
        mixed = jnp.sum(t_r[slot * ny : (slot + 1) * ny].astype(F32), axis=0)
        hbuf[y, slot] = ((residual[slot] + mixed) * gain).astype(BF16)
    offsets = sorted(range(1 - half // 2, half // 2 + 1), key=abs)
    for k in range(half - 1, 0, -1):
        send(19 + k, hbuf.at[y], hbuf.at[y], (ctx, (y + ny + offsets[k]) % ny))
    bytes_of(0, tbuf.at[0 : plane - 1]).wait_recv()

    span = width // 4
    blocks = span // LANES
    pair = iota((8, LANES), 0) // 2
    for k, slot in [(k, slot) for k in range(half) for slot in range(2)]:
        if k and slot == 0:
            bytes_of(19 + k, hbuf.at[0]).wait_recv()
        owner = (y + ny - offsets[k]) % ny
        group = (owner + slot * half) % ny
        gathered = hbuf[owner, slot].astype(F32)
        halves = [gathered[:8], gathered[8:]]
        plain = [halves[0] / own[0:1], halves[1] / other[0:1]]
        squares = jnp.sum(plain[0] * plain[0] + plain[1] * plain[1], axis=1, keepdims=True)
        x = jnp.concatenate(halves, axis=1)
        turned = jnp.concatenate([roll_rows(x, 2 * q) for q in range(4)], axis=0).astype(BF16)
        product = dot(turned, vwbuf[...])
        marks = tbuf[pl.ds(group * 4, 4)]
        target = jnp.concatenate([marks[u] for u in range(4)], axis=0)
        logits = []
        picked = jnp.zeros((8, 1), F32)
        for q in range(4):
            part = product[8 * q : 8 * q + 8, q * span : (q + 1) * span]
            column = y * width + q * span + iota((8, span), 1)
            wanted = roll_rows(target, 2 * q)[:, 0:1]
            found = jnp.sum(jnp.where(column == wanted, part, 0.0), axis=1, keepdims=True)
            picked = picked + roll_rows(found, -2 * q)
            logits.append(part)
        both = jnp.where(iota((8, LANES), 1) < 64, squares, picked)
        for u in range(4):
            pieces = []
            for b in range(blocks):
                cut = [part[:, b * LANES : (b + 1) * LANES] for part in logits]
                piece = cut[(u - 3) % 4]
                for p in range(3):
                    piece = jnp.where(pair == p, cut[(u - p) % 4], piece)
                pieces.append(piece)
            l_s[group, u] = jnp.concatenate(pieces, axis=0).astype(BF16)
            to = group * 4 + u
            s2_s[to] = both[2 * u : 2 * u + 2]

            @pl.when(to != me)
            def _(u=u, to=to, group=group):
                peer = (2 * to + core, y)
                send(13, l_s.at[group, u], l_r.at[me], peer)
                send(14, s2_s.at[to], s2_r.at[me], peer)

    l_r[me] = l_s[me // 4, me % 4]
    s2_r[me] = s2_s[me]
    bytes_of(13, l_r.at[0 : plane - 1]).wait_recv()
    bytes_of(14, s2_r.at[0 : plane - 1]).wait_recv()

    total = jnp.sum(l_r[...].astype(F32), axis=0)
    both = jnp.sum(s2_r[...], axis=0)
    both = jnp.concatenate([both] * 4, axis=0)
    inverse = lax.rsqrt(both[:, 0:1] / features + EPS)
    picked = both[:, 64:65] * inverse
    logit = total.reshape(-1, 8, LANES) * inverse

    def around_pairs(x, join):
        x = jnp.broadcast_to(x, (8, LANES))
        for shift in (2, 4):
            x = join(x, pltpu.roll(x, shift, 0))
        return x

    top = around_pairs(jnp.max(jnp.max(logit, axis=0), axis=1, keepdims=True), jnp.maximum)
    sums = jnp.sum(jnp.sum(jnp.exp(logit - top), axis=0), axis=1, keepdims=True)
    sums = around_pairs(sums, jnp.add)
    lane8 = iota((8, LANES), 1)
    f_r[y] = jnp.where(lane8 < 32, top, jnp.where(lane8 < 64, sums, picked))
    for _, peer in y_peers:
        send(15, f_r.at[y], f_r.at[y], peer)
    for dx in range(nx):
        bytes_of(16 + dx, qbuf.at[0 : nz - (dx == 0)]).wait_send()
        bytes_of(4 if dx == 0 else 27 + dx, abuf.at[0 : nz - (dx == 0)]).wait_send()
    for k in range(1, half):
        bytes_of(19 + k, hbuf.at[0]).wait_send()
    bytes_of(1, misc.at[1]).wait_send()
    bytes_of(2, kbuf.at[1]).wait_send()
    bytes_of(3, vbuf.at[1]).wait_send()
    bytes_of(0, tbuf.at[0 : plane - 1]).wait_send()
    bytes_of(5, resbuf.at[1]).wait_send()
    bytes_of(6, wbuf.at[1]).wait_send()
    bytes_of(7, vwbuf.at[0:LANES]).wait_send()
    bytes_of(8, st_r.at[0 : plane - 1]).wait_send()
    bytes_of(9, acc_r.at[0 : plane - 1]).wait_send()
    bytes_of(11, t_r.at[0 : 2 * (ny - 1)]).wait_send()
    bytes_of(13, l_r.at[0 : plane - 1]).wait_send()
    bytes_of(14, s2_r.at[0 : plane - 1]).wait_send()
    bytes_of(15, f_r.at[0 : ny - 1]).wait_recv()
    final = f_r[...]
    tops = final[:, :, 0:1]
    top = jnp.max(tops, axis=0)
    sums = jnp.sum(final[:, :, 32:33] * jnp.exp(tops - top), axis=0)
    lse = top + jnp.log(sums)
    picked = jnp.sum(final[:, :, 64:65], axis=0)
    out_ref[...] = jnp.where(lane8 < 64, lse, picked)

    bytes_of(15, f_r.at[0 : ny - 1]).wait_send()


def body(plane, ny, *args):
    (
        queries,
        cache_keys,
        cache_values,
        reply_keys,
        reply_values,
        block_prompt,
        lengths,
        residual,
        norm_gain,
        out_weight,
        vocab_weight,
        targets,
    ) = args
    width = vocab_weight.shape[1]
    keys = cache_keys.shape[0]
    hbm = pl.BlockSpec(memory_space=pltpu.HBM)
    vmem = pltpu.VMEM
    out = pl.pallas_call(
        functools.partial(kernel, plane, ny, width),
        out_shape=jax.ShapeDtypeStruct((8, LANES), F32),
        in_specs=[hbm] * len(args),
        out_specs=pl.BlockSpec(memory_space=pltpu.VMEM),
        scratch_shapes=[
            vmem(queries.shape, BF16),
            vmem(reply_keys.shape, BF16),
            vmem(reply_values.shape, BF16),
            vmem((1, LANES), F32),
            pltpu.SMEM(block_prompt.shape, jnp.int32),
            pltpu.SMEM(lengths.shape, jnp.int32),
            pltpu.SMEM(targets.shape, jnp.int32),
            vmem((2, keys, HD), BF16),
            vmem((2, keys, HD), BF16),
            vmem((2,) + residual.shape, BF16),
            vmem((2,) + out_weight.shape, BF16),
            vmem((2 * LANES, width), BF16),
            vmem((2, 8, LANES), F32),
            vmem((plane, 16, HD), BF16),
            vmem((2, LANES), jnp.int32),
            vmem((plane, 2, LANES), jnp.int32),
            vmem((plane, 16, HD), BF16),
            vmem((plane, 16, HD), BF16),
            vmem((plane, 2, LANES), F32),
            vmem((plane, 2, LANES), F32),
            vmem((plane, 16, HD), BF16),
            vmem((ny, 16, LANES), BF16),
            vmem((2 * ny, 16, LANES), BF16),
            vmem((ny, 2, 16, LANES), BF16),
            vmem((plane // 4, 4, 2 * width // LANES, LANES), BF16),
            vmem((plane, 2 * width // LANES, LANES), BF16),
            vmem((plane, 2, LANES), F32),
            vmem((plane, 2, LANES), F32),
            vmem((ny, 8, LANES), F32),
            pltpu.SemaphoreType.DMA((12,)),
            pltpu.SemaphoreType.DMA((32,)),
            pltpu.SemaphoreType.DMA((32,)),
        ],
        compiler_params=pltpu.CompilerParams(
            collective_id=0, has_side_effects=True, vmem_limit_bytes=60 * 2**20
        ),
    )(
        queries,
        cache_keys,
        cache_values,
        reply_keys,
        reply_values,
        block_prompt,
        lengths,
        residual,
        norm_gain.reshape(1, LANES),
        out_weight,
        vocab_weight,
        targets,
    )
    return out[0:2, 0], out[0:2, 64]


def solution(mesh):
    plane, ny = mesh.shape["ctx"] // 2, mesh.shape["tp"]
    return jax.shard_map(
        functools.partial(body, plane, ny),
        mesh=mesh,
        in_specs=(
            P("ctx", "tp"),
            P("ctx", "tp"),
            P("ctx", "tp"),
            P("ctx", "tp"),
            P("ctx", "tp"),
            P("ctx"),
            P(),
            P(None, "ctx"),
            P("ctx"),
            P("tp", "ctx"),
            P("ctx", "tp"),
            P("ctx"),
        ),
        out_specs=(P("ctx"), P("ctx")),
        check_vma=False,
    )
```

```python
import functools

import jax
import jax.numpy as jnp
from jax import lax
from jax.experimental import pallas as pl
from jax.experimental.pallas import tpu as pltpu
from jax.sharding import PartitionSpec as P

MESH = pl.DeviceIdType.MESH
F32 = jnp.float32
BF16 = jnp.bfloat16

HD = 128
HEADS = 8
NEG = -1e30
EPS = 1e-06
LOG2E = 1.4426950408889634
LANES = 128
CHUNK = 128


def iota(shape, dim):
    return lax.broadcasted_iota(jnp.int32, shape, dim)


def dot(a, b):
    return jnp.dot(a, b, preferred_element_type=F32)


def dot_t(a, b):
    return lax.dot_general(a, b, (((1,), (1,)), ((), ())), preferred_element_type=F32)


def roll_rows(x, shift):
    shift = shift % 8
    return jnp.concatenate([x[shift:], x[:shift]], axis=0) if shift else x


def kernel(
    plane,
    ny,
    width,
    q_hbm,
    k_hbm,
    v_hbm,
    rk_hbm,
    rv_hbm,
    bp_hbm,
    len_hbm,
    res_hbm,
    gain_hbm,
    w_hbm,
    vw_hbm,
    tgt_hbm,
    out_ref,
    q_in,
    rk_in,
    rv_in,
    gain_in,
    bp_smem,
    len_smem,
    tgt_smem,
    kbuf,
    vbuf,
    resbuf,
    wbuf,
    vwbuf,
    misc,
    qbuf,
    tsrc,
    tbuf,
    acc_s,
    acc_r,
    st_s,
    st_r,
    abuf,
    t_s,
    t_r,
    hbuf,
    l_s,
    l_r,
    s2_s,
    s2_r,
    f_r,
    local_sem,
    send_sem,
    recv_sem,
):
    ctx = lax.axis_index("ctx")
    y = lax.axis_index("tp")
    core = ctx % 2
    me = ctx // 2
    partner = (ctx + 1 - 2 * core, y)
    nctx = 2 * plane
    qrows = 16 * plane
    features = nctx * LANES
    c1 = (HD ** (-0.5)) * LOG2E

    nz = 8
    nx = plane // nz
    along_x = [((me // nz + dx) % nx) * nz for dx in range(nx)]
    along_z = [(me % nz + dz) % nz for dz in range(nz)]
    steps = [(dx, dz) for dx in range(nx) for dz in range(nz) if dx or dz]
    steps.sort(key=lambda s: -min(s[0], nx - s[0]) - min(s[1], nz - s[1]))
    plane_to = [along_x[dx] + along_z[dz] for dx, dz in steps]
    plane_peers = [(to, (2 * to + core, y)) for to in plane_to]
    y_steps = sorted(range(1, ny), key=lambda s: -min(s, ny - s))
    y_peers = [((y + k) % ny, (ctx, (y + k) % ny)) for k in y_steps]

    barrier = pltpu.get_barrier_semaphore()
    greeted = [device for _, device in plane_peers + y_peers] + [partner]
    for peer in greeted:
        pl.semaphore_signal(barrier, inc=1, device_id=peer, device_id_type=MESH)

    def local(index, src, dst):
        copy = pltpu.make_async_copy(src, dst, local_sem.at[index])
        copy.start()
        return copy

    copies = [
        local(0, q_hbm, q_in),
        local(1, rk_hbm, rk_in),
        local(2, rv_hbm, rv_in),
        local(3, gain_hbm, gain_in),
        local(9, bp_hbm, bp_smem),
        local(10, len_hbm, len_smem),
        local(11, tgt_hbm, tgt_smem),
    ]
    big = [
        local(4, k_hbm, kbuf.at[0]),
        local(5, v_hbm, vbuf.at[0]),
        local(6, res_hbm, resbuf.at[0]),
        local(7, w_hbm, wbuf.at[0]),
        local(8, vw_hbm, vwbuf.at[0:LANES]),
    ]
    for copy in copies:
        copy.wait()

    def send(index, src, dst, peer):
        pltpu.make_async_remote_copy(
            src_ref=src,
            dst_ref=dst,
            send_sem=send_sem.at[index],
            recv_sem=recv_sem.at[index],
            device_id=peer,
            device_id_type=MESH,
        ).start()

    def bytes_of(index, ref):
        return pltpu.make_async_remote_copy(
            src_ref=ref,
            dst_ref=ref,
            send_sem=send_sem.at[index],
            recv_sem=recv_sem.at[index],
            device_id=partner,
            device_id_type=MESH,
        )

    qf = q_in[...].astype(F32)
    tile = jnp.concatenate([qf[:, h * HD : (h + 1) * HD] for h in range(HEADS)], axis=0)
    qbuf[me] = tile.astype(BF16)
    misc[0, 0:1, :] = gain_in[...]
    misc[0, 1:2, :] = jnp.full((1, LANES), bp_smem[0], jnp.int32).astype(F32)
    misc[0, 2:4, :] = rk_in[...].astype(F32)
    misc[0, 4:6, :] = rv_in[...].astype(F32)
    misc[0, 6:8, :] = jnp.zeros((2, LANES), F32)
    two = iota((2, LANES), 0)
    tsrc[...] = jnp.where(two == 0, tgt_smem[0], tgt_smem[1])
    tbuf[me] = tsrc[...]

    pl.semaphore_wait(barrier, len(greeted))

    for (dx, _), (_, peer) in zip(steps, plane_peers):
        send(16 + dx, qbuf.at[me], qbuf.at[me], peer)
    send(1, misc.at[0], misc.at[1], partner)
    send(2, k_hbm, kbuf.at[1], partner)
    send(3, v_hbm, vbuf.at[1], partner)
    send(5, res_hbm, resbuf.at[1], partner)
    send(6, w_hbm, wbuf.at[1], partner)
    send(7, vw_hbm, vwbuf.at[LANES : 2 * LANES], partner)

    into = iota((nz * 16, nz * 16), 0)
    source = (into // 2 % nz) * 16 + (into // (2 * nz)) * 2 + into % 2
    perm = jnp.where(iota((nz * 16, nz * 16), 1) == source, 1.0, 0.0).astype(BF16)

    end0 = len_smem[0]
    end1 = end0 + len_smem[1]
    end2 = end1 + len_smem[2]

    def segment(index):
        one = lambda end: jnp.where(index >= end, 1, 0)
        return one(end0) + one(end1) + one(end2) + one(end2 + len_smem[3])

    for copy in big:
        copy.wait()
    bytes_of(1, misc.at[1]).wait_recv()
    bytes_of(2, kbuf.at[1]).wait_recv()
    bytes_of(3, vbuf.at[1]).wait_recv()

    own, other = misc[0], misc[1]
    fill = jnp.zeros((LANES - 4, HD), F32)
    rk = jnp.concatenate([own[2:4], other[2:4], fill], axis=0).astype(BF16)
    rv = jnp.concatenate([own[4:6], other[4:6], fill], axis=0).astype(BF16)
    prompts = (own[1:2, 0:1], other[1:2, 0:1])
    lane = iota((CHUNK, LANES), 1)
    key_row = jnp.where(lane < 2, 2 * ctx + lane, 2 * (ctx + 1 - 2 * core) + lane - 2)
    key_segment = segment(key_row)

    tiles = CHUNK // 16

    def attend(at):
        first = at * 16
        q = qbuf[pl.ds(at, tiles)].reshape(CHUNK, HD)
        n = first + iota((CHUNK, LANES), 0)
        row = 4 * (n // 16) + 2 * core + n % 2
        row_segment = segment(row)
        row_prompt = (row_segment // 2).astype(F32)
        allowed = (lane < 4) & (key_segment == row_segment) & (key_row <= row)
        reply = jnp.where(allowed, dot_t(q, rk), NEG)
        scores = [dot_t(q, kbuf[block]) for block in range(2)]
        reply_top = jnp.max(reply, axis=1, keepdims=True)
        tops = [jnp.max(s, axis=1, keepdims=True) for s in scores]
        p = jnp.where(allowed, jnp.exp2((reply - reply_top) * c1), 0.0)
        parts = [(reply_top, jnp.sum(p, axis=1, keepdims=True), dot(p.astype(BF16), rv))]
        for block in range(2):
            p = jnp.exp2((scores[block] - tops[block]) * c1)
            total = jnp.sum(p, axis=1, keepdims=True)
            acc = dot(p.astype(BF16), vbuf[block])
            m = jnp.where(row_prompt == prompts[block], tops[block], NEG)
            parts.append((m, total, acc))
        top = jnp.maximum(jnp.maximum(parts[0][0], parts[1][0]), parts[2][0])
        total = jnp.zeros((CHUNK, LANES), F32)
        acc = jnp.zeros((CHUNK, HD), F32)
        for m, t, a in parts:
            w = jnp.exp2((m - top) * c1)
            total = total + w * t
            acc = acc + w * a
        acc_s[pl.ds(at, tiles)] = acc.astype(BF16).reshape(tiles, 16, HD)
        here = lane == (me % 8) * 16 + n % 16
        for which, stat in ((0, top), (1, total)):
            packed = jnp.where(here, stat, 0.0).reshape(tiles, 16, LANES)
            st_s[pl.ds(at, tiles), which : which + 1, :] = jnp.sum(
                packed, axis=1, keepdims=True
            )

    for dx in sorted(range(nx), key=lambda d: min(d, nx - d) if d != nx - 1 else nx):
        bytes_of(16 + dx, qbuf.at[0 : nz - (dx == 0)]).wait_recv()
        attend(along_x[(nx - dx) % nx])
        for (back, _), (to, peer) in zip(steps, plane_peers):
            if back == (nx - dx) % nx:
                send(8, st_s.at[to], st_r.at[me], peer)
                send(9, acc_s.at[to], acc_r.at[me], peer)
    acc_r[me] = acc_s[me]
    st_r[me] = st_s[me]

    half = ny // 2
    bytes_of(5, resbuf.at[1]).wait_recv()
    into = iota((16, 32), 0)
    inner = into % 8
    source = (into // 8) * 16 + 4 * (inner // 2) + 2 * core + inner % 2
    pick = jnp.where(iota((16, 32), 1) == source, 1.0, 0.0).astype(BF16)
    residual = []
    for group in (y, (y + half) % ny):
        at = pl.multiple_of(group * 16, 16)
        around = [resbuf[side, pl.ds(at, 16), :] for side in range(2)]
        residual.append(dot(pick, jnp.concatenate(around, axis=0)))
    upper = iota((16, LANES), 0) < 8
    gain = jnp.where(upper, own[0:1], other[0:1])

    bytes_of(8, st_r.at[0 : plane - 1]).wait_recv()
    bytes_of(9, acc_r.at[0 : plane - 1]).wait_recv()

    stats = [jnp.sum(st_r[x * 8 : (x + 1) * 8], axis=0) for x in range(plane // 8)]
    m = jnp.concatenate([s[0:1] for s in stats], axis=0)
    total = jnp.concatenate([s[1:2] for s in stats], axis=0)

    def around_lanes(x, join):
        for shift in (16, 32, 64):
            x = join(x, pltpu.roll(x, shift, 1))
        return x

    top = around_lanes(jnp.max(m, axis=0, keepdims=True), jnp.maximum)
    w = jnp.exp2((m - top) * c1)
    total = around_lanes(jnp.sum(w * total, axis=0, keepdims=True), jnp.add)
    w = w / total
    diagonal = iota((16, LANES), 1) % 16 == iota((16, LANES), 0)
    w = jnp.concatenate(
        [jnp.where(diagonal, w[x : x + 1], 0.0) for x in range(plane // 8)], axis=1
    )
    high = w.astype(BF16)
    low = (w - high.astype(F32)).astype(BF16)
    partials = acc_r[...].reshape(qrows, HD)
    attention = dot(high, partials) + dot(low, partials)
    abuf[me] = attention.astype(BF16)
    for (dx, _), (_, peer) in zip(steps, plane_peers):
        send(4 if dx == 0 else 27 + dx, abuf.at[me], abuf.at[me], peer)
    for _, peer in plane_peers:
        send(0, tsrc, tbuf.at[me], peer)
    bytes_of(6, wbuf.at[1]).wait_recv()
    bytes_of(7, vwbuf.at[0:LANES]).wait_recv()

    share = ny // nx
    for dx in sorted(range(nx), key=lambda d: min(d, nx - d)):
        bytes_of(4 if dx == 0 else 27 + dx, abuf.at[0 : nz - (dx == 0)]).wait_recv()
        at = along_x[(nx - dx) % nx]
        heads = dot(perm, abuf[pl.ds(at, nz)].reshape(nz * 16, HD)).astype(BF16)
        span = 2 * nz
        heads = jnp.concatenate([heads[h * span : (h + 1) * span] for h in range(HEADS)], axis=1)
        terms = [dot(heads, wbuf[half]).reshape(share, 8, LANES) for half in range(2)]
        to = at // nz * share
        t_s[pl.ds(to, share)] = jnp.concatenate(terms, axis=1).astype(BF16)
        for k in range(share):
            for slot in range(2):
                owner = (to + k + slot * half) % ny

                @pl.when(owner != y)
                def _(group=to + k, slot=slot, owner=owner):
                    send(11, t_s.at[group], t_r.at[slot * ny + y], (ctx, owner))

    for slot in range(2):
        t_r[slot * ny + y] = t_s[(y + slot * half) % ny]
    bytes_of(11, t_r.at[0 : 2 * (ny - 1)]).wait_recv()
    for slot in range(2):
        mixed = jnp.sum(t_r[slot * ny : (slot + 1) * ny].astype(F32), axis=0)
        hbuf[y, slot] = ((residual[slot] + mixed) * gain).astype(BF16)
    offsets = sorted(range(1 - half // 2, half // 2 + 1), key=abs)
    for k in range(half - 1, 0, -1):
        send(19 + k, hbuf.at[y], hbuf.at[y], (ctx, (y + ny + offsets[k]) % ny))
    bytes_of(0, tbuf.at[0 : plane - 1]).wait_recv()

    span = width // 4
    blocks = span // LANES
    pair = iota((8, LANES), 0) // 2
    for k, slot in [(k, slot) for k in range(half) for slot in range(2)]:
        if k and slot == 0:
            bytes_of(19 + k, hbuf.at[0]).wait_recv()
        owner = (y + ny - offsets[k]) % ny
        group = (owner + slot * half) % ny
        gathered = hbuf[owner, slot].astype(F32)
        halves = [gathered[:8], gathered[8:]]
        plain = [halves[0] / own[0:1], halves[1] / other[0:1]]
        squares = jnp.sum(plain[0] * plain[0] + plain[1] * plain[1], axis=1, keepdims=True)
        x = jnp.concatenate(halves, axis=1)
        turned = jnp.concatenate([roll_rows(x, 2 * q) for q in range(4)], axis=0).astype(BF16)
        product = dot(turned, vwbuf[...])
        marks = tbuf[pl.ds(group * 4, 4)]
        target = jnp.concatenate([marks[u] for u in range(4)], axis=0)
        logits = []
        picked = jnp.zeros((8, 1), F32)
        for q in range(4):
            part = product[8 * q : 8 * q + 8, q * span : (q + 1) * span]
            column = y * width + q * span + iota((8, span), 1)
            wanted = roll_rows(target, 2 * q)[:, 0:1]
            found = jnp.sum(jnp.where(column == wanted, part, 0.0), axis=1, keepdims=True)
            picked = picked + roll_rows(found, -2 * q)
            logits.append(part)
        both = jnp.where(iota((8, LANES), 1) < 64, squares, picked)
        for u in range(4):
            pieces = []
            for b in range(blocks):
                cut = [part[:, b * LANES : (b + 1) * LANES] for part in logits]
                piece = cut[(u - 3) % 4]
                for p in range(3):
                    piece = jnp.where(pair == p, cut[(u - p) % 4], piece)
                pieces.append(piece)
            l_s[group, u] = jnp.concatenate(pieces, axis=0).astype(BF16)
            to = group * 4 + u
            s2_s[to] = both[2 * u : 2 * u + 2]

            @pl.when(to != me)
            def _(u=u, to=to, group=group):
                peer = (2 * to + core, y)
                send(13, l_s.at[group, u], l_r.at[me], peer)
                send(14, s2_s.at[to], s2_r.at[me], peer)

    l_r[me] = l_s[me // 4, me % 4]
    s2_r[me] = s2_s[me]
    bytes_of(13, l_r.at[0 : plane - 1]).wait_recv()
    bytes_of(14, s2_r.at[0 : plane - 1]).wait_recv()

    total = jnp.sum(l_r[...].astype(F32), axis=0)
    both = jnp.sum(s2_r[...], axis=0)
    both = jnp.concatenate([both] * 4, axis=0)
    inverse = lax.rsqrt(both[:, 0:1] / features + EPS)
    picked = both[:, 64:65] * inverse
    logit = total.reshape(-1, 8, LANES) * inverse

    def around_pairs(x, join):
        x = jnp.broadcast_to(x, (8, LANES))
        for shift in (2, 4):
            x = join(x, pltpu.roll(x, shift, 0))
        return x

    top = around_pairs(jnp.max(jnp.max(logit, axis=0), axis=1, keepdims=True), jnp.maximum)
    sums = jnp.sum(jnp.sum(jnp.exp(logit - top), axis=0), axis=1, keepdims=True)
    sums = around_pairs(sums, jnp.add)
    lane8 = iota((8, LANES), 1)
    f_r[y] = jnp.where(lane8 < 32, top, jnp.where(lane8 < 64, sums, picked))
    for _, peer in y_peers:
        send(15, f_r.at[y], f_r.at[y], peer)
    for dx in range(nx):
        bytes_of(16 + dx, qbuf.at[0 : nz - (dx == 0)]).wait_send()
        bytes_of(4 if dx == 0 else 27 + dx, abuf.at[0 : nz - (dx == 0)]).wait_send()
    for k in range(1, half):
        bytes_of(19 + k, hbuf.at[0]).wait_send()
    bytes_of(1, misc.at[1]).wait_send()
    bytes_of(2, kbuf.at[1]).wait_send()
    bytes_of(3, vbuf.at[1]).wait_send()
    bytes_of(0, tbuf.at[0 : plane - 1]).wait_send()
    bytes_of(5, resbuf.at[1]).wait_send()
    bytes_of(6, wbuf.at[1]).wait_send()
    bytes_of(7, vwbuf.at[0:LANES]).wait_send()
    bytes_of(8, st_r.at[0 : plane - 1]).wait_send()
    bytes_of(9, acc_r.at[0 : plane - 1]).wait_send()
    bytes_of(11, t_r.at[0 : 2 * (ny - 1)]).wait_send()
    bytes_of(13, l_r.at[0 : plane - 1]).wait_send()
    bytes_of(14, s2_r.at[0 : plane - 1]).wait_send()
    bytes_of(15, f_r.at[0 : ny - 1]).wait_recv()
    final = f_r[...]
    tops = final[:, :, 0:1]
    top = jnp.max(tops, axis=0)
    sums = jnp.sum(final[:, :, 32:33] * jnp.exp(tops - top), axis=0)
    lse = top + jnp.log(sums)
    picked = jnp.sum(final[:, :, 64:65], axis=0)
    out_ref[...] = jnp.where(lane8 < 64, lse, picked)

    bytes_of(15, f_r.at[0 : ny - 1]).wait_send()


def body(plane, ny, *args):
    (
        queries,
        cache_keys,
        cache_values,
        reply_keys,
        reply_values,
        block_prompt,
        lengths,
        residual,
        norm_gain,
        out_weight,
        vocab_weight,
        targets,
    ) = args
    width = vocab_weight.shape[1]
    keys = cache_keys.shape[0]
    hbm = pl.BlockSpec(memory_space=pltpu.HBM)
    vmem = pltpu.VMEM
    out = pl.pallas_call(
        functools.partial(kernel, plane, ny, width),
        out_shape=jax.ShapeDtypeStruct((8, LANES), F32),
        in_specs=[hbm] * len(args),
        out_specs=pl.BlockSpec(memory_space=pltpu.VMEM),
        scratch_shapes=[
            vmem(queries.shape, BF16),
            vmem(reply_keys.shape, BF16),
            vmem(reply_values.shape, BF16),
            vmem((1, LANES), F32),
            pltpu.SMEM(block_prompt.shape, jnp.int32),
            pltpu.SMEM(lengths.shape, jnp.int32),
            pltpu.SMEM(targets.shape, jnp.int32),
            vmem((2, keys, HD), BF16),
            vmem((2, keys, HD), BF16),
            vmem((2,) + residual.shape, BF16),
            vmem((2,) + out_weight.shape, BF16),
            vmem((2 * LANES, width), BF16),
            vmem((2, 8, LANES), F32),
            vmem((plane, 16, HD), BF16),
            vmem((2, LANES), jnp.int32),
            vmem((plane, 2, LANES), jnp.int32),
            vmem((plane, 16, HD), BF16),
            vmem((plane, 16, HD), BF16),
            vmem((plane, 2, LANES), F32),
            vmem((plane, 2, LANES), F32),
            vmem((plane, 16, HD), BF16),
            vmem((ny, 16, LANES), BF16),
            vmem((2 * ny, 16, LANES), BF16),
            vmem((ny, 2, 16, LANES), BF16),
            vmem((plane // 4, 4, 2 * width // LANES, LANES), BF16),
            vmem((plane, 2 * width // LANES, LANES), BF16),
            vmem((plane, 2, LANES), F32),
            vmem((plane, 2, LANES), F32),
            vmem((ny, 8, LANES), F32),
            pltpu.SemaphoreType.DMA((12,)),
            pltpu.SemaphoreType.DMA((32,)),
            pltpu.SemaphoreType.DMA((32,)),
        ],
        compiler_params=pltpu.CompilerParams(
            collective_id=0, has_side_effects=True, vmem_limit_bytes=60 * 2**20
        ),
    )(
        queries,
        cache_keys,
        cache_values,
        reply_keys,
        reply_values,
        block_prompt,
        lengths,
        residual,
        norm_gain.reshape(1, LANES),
        out_weight,
        vocab_weight,
        targets,
    )
    return out[0:2, 0], out[0:2, 64]


def solution(mesh):
    plane, ny = mesh.shape["ctx"] // 2, mesh.shape["tp"]
    return jax.shard_map(
        functools.partial(body, plane, ny),
        mesh=mesh,
        in_specs=(
            P("ctx", "tp"),
            P("ctx", "tp"),
            P("ctx", "tp"),
            P("ctx", "tp"),
            P("ctx", "tp"),
            P("ctx"),
            P(),
            P(None, "ctx"),
            P("ctx"),
            P("tp", "ctx"),
            P("ctx", "tp"),
            P("ctx"),
        ),
        out_specs=(P("ctx"), P("ctx")),
        check_vma=False,
    )
```
